128 devices in a mesh: dp: 32 (over y, x, core), tensor: 4 (over z).
Axes of the slice: x: 4, y: 4, z: 4, core: 2. Of those that a mesh axis runs over, the one named last changes fastest.
Arguments:
- hidden_states: bfloat16 [12288, 8192], P('dp'), may hold values from -6 to 6
- teacher_weight: bfloat16 [8192, 4096], P('dp', 'tensor'), may hold values from -0.088388348 to 0.088388348
- student_blocks: bfloat16 [192, 4, 128, 128], P('dp', 'tensor'), may hold values from -0.125 to 0.125
- block_index: int32 [192, 4], P('dp', 'tensor'), may hold values from -1 to 15, as said below
Outputs:
- block_grads: float32 [192, 4, 128, 128], P('dp', 'tensor')
- input_grad: bfloat16 [12288, 8192], P('dp', 'tensor')
The draws below stay inside these ranges and needn't reach their ends.
Inputs may be any that keep to these rules, and one draw needn't show every extreme that they name: `block_index`: entries (i * 6 + s, j) for s < 6 form one shard's list: its live entries are distinct block numbers of the shard's 2 x 8 blocks, they come first and the rest are -1; every shard has 3 to 6 live entries, and in every draw some shard has exactly 6.
All inputs are finite; a program needn't handle non-finite values.
Results may differ from the reference program's by a relative error of at most 0.014.
Values may be sent and summed in bfloat16 or wider, within the bound.
A program may use at most 192 MiB of HBM per device.

```python
import math
import jax
import jax.numpy as jnp
from jax import lax

D = 8192
BLK = 128
TOK_DEV = 384
QW = 4096
TOKENS = 12288
SLOTS = 16
CAP = 6
BLOCKS = 192
N_DP = 32
N_TENSOR = 4


def draw_teacher_weight(key, part):
    key = jax.random.fold_in(key, 11)
    position = jnp.arange(QW, dtype=jnp.float32) / QW
    raw = jnp.clip(jax.random.normal(key, (D, QW), jnp.float32), -6.0, 6.0)
    scale = jnp.sqrt(0.5 + position)
    return (raw * scale[None, :] / math.sqrt(D)).astype(jnp.bfloat16)


def draw_block_index(key, part):
    key = jax.random.fold_in(key, 7)
    first, second, third = jax.random.split(key, 3)
    shard_count = N_DP * N_TENSOR
    keys = jax.random.split(first, shard_count)
    orders = jax.vmap(lambda k: jax.random.permutation(k, SLOTS))(keys)[:, :CAP]
    counts = jax.random.randint(second, (shard_count,), CAP // 2, CAP + 1)
    fullest = jax.random.randint(third, (), 0, shard_count)
    counts = jnp.where(jnp.arange(shard_count) == fullest, CAP, counts)
    alive = jnp.arange(CAP)[None, :] < counts[:, None]
    listed = jnp.where(alive, orders, -1)
    return listed.reshape(N_DP, N_TENSOR, CAP).transpose(0, 2, 1).reshape(N_DP * CAP, N_TENSOR).astype(jnp.int32)


def with_spikes(drawn, rng, source, target, blocks, factor):
    owner, partner = [(jnp.arange(drawn.shape[axis_at]) // (drawn.shape[axis_at] // blocks)).reshape([-1 if axis == axis_at else 1 for axis in range(drawn.ndim)]) for axis_at in (source, target)]
    chosen = jax.random.permutation(rng, blocks)[partner]
    strong = (owner == chosen) | (owner == (partner + blocks // 2) % blocks)
    return jnp.where(strong, factor * drawn, drawn)


def steps_of(rng, shape, cuts, smallest, largest):
    def one(axis_at, parts):
        steps = jax.random.uniform(jax.random.fold_in(jax.random.fold_in(rng, 6), axis_at), (parts,), jnp.float32, smallest / len(cuts), largest / len(cuts))
        return jnp.repeat(jnp.exp(steps), shape[axis_at] // parts).reshape((-1,) + (1,) * (len(shape) - axis_at - 1))

    loudness = one(*cuts[0])
    for cut in cuts[1:]:
        loudness = loudness * one(*cut)
    return loudness


def noise(stream_key, dims, scale, reach, cuts=(), held_as=jnp.bfloat16):
    values = jax.random.normal(stream_key, dims, jnp.float32) * scale
    if len(cuts) > 0:
        values = steps_of(stream_key, dims, cuts, -0.22, 0.18) * values
    return jnp.clip(values, min=-reach, max=reach).astype(held_as)


def bell_draw_with(stream_key, dims, deviation, reach, cuts, heavy, held_as=jnp.bfloat16):
    entries = deviation * jax.random.normal(stream_key, dims, jnp.float32)
    if cuts:
        entries = entries * steps_of(stream_key, dims, cuts, -0.22, 0.18)
    return jnp.clip(with_spikes(entries, jax.random.fold_in(stream_key, 3), *heavy), -reach, reach).astype(held_as)


def setup_inputs(seed: int = 0) -> dict:
    key_of = jax.random.split(jax.random.key(seed), 5)
    hidden_states = bell_draw_with(key_of[0], (TOKENS, D), 1.0, 6.0, ((0, 32),), (0, 1, 32, 2.75))
    teacher_weight = draw_teacher_weight(jax.random.fold_in(key_of[4], 71), 0)
    student_blocks = noise(key_of[2], (BLOCKS, N_TENSOR, BLK, BLK), (D * 3 // 10) ** -0.5, 0.125, ((0, 32), (1, 4)))
    block_index = draw_block_index(jax.random.fold_in(key_of[4], 71), 0)
    return {"hidden_states": hidden_states, "teacher_weight": teacher_weight, "student_blocks": student_blocks, "block_index": block_index}


def scatter_blocks(values, index, shards, row_blocks, col_blocks, per_shard):
    size = values.shape[-1]
    live = index >= 0
    safe = jnp.maximum(index, 0)
    owner = jnp.arange(index.shape[0], dtype=jnp.int32) // per_shard
    rows = owner * row_blocks + safe // col_blocks
    cols = safe % col_blocks
    masked = jnp.where(live[:, None, None], values, jnp.zeros_like(values))
    grid = jnp.zeros((shards * row_blocks, size, col_blocks, size), values.dtype)
    grid = grid.at[rows, :, cols, :].add(masked)
    return grid.reshape(shards * row_blocks * size, col_blocks * size)

def reference(hidden_states, teacher_weight, student_blocks, block_index):
    row_blocks = D // (N_DP * BLK)
    col_blocks = QW // (N_TENSOR * BLK)
    local_width = QW // N_TENSOR
    slabs = [scatter_blocks(student_blocks[:, j], block_index[:, j], N_DP, row_blocks, col_blocks, CAP) for j in range(N_TENSOR)]
    teacher_out = jnp.dot(hidden_states, teacher_weight, preferred_element_type=jnp.float32)
    student_out = jnp.concatenate([jnp.dot(hidden_states, slab, preferred_element_type=jnp.float32) for slab in slabs], axis=1)
    squares = lax.optimization_barrier(jnp.sum(teacher_out * teacher_out, axis=1))
    weight = 1.0 / (squares / QW + 1e-05)
    scale = 1.0 / math.sqrt(TOKENS)
    grad_out = (weight[:, None] * (student_out - teacher_out) * scale).astype(jnp.bfloat16)
    total = jnp.zeros((TOKENS, D), jnp.float32)
    for j in range(N_TENSOR):
        part = jnp.dot(grad_out[:, j * local_width:(j + 1) * local_width], slabs[j].T, preferred_element_type=jnp.float32)
        part = lax.optimization_barrier(part.astype(jnp.bfloat16)).astype(jnp.float32)
        total = total + part
    input_grad = total.astype(jnp.bfloat16)
    inputs4 = hidden_states.reshape(N_DP, TOK_DEV, D // BLK, BLK)
    grads4 = grad_out.reshape(N_DP, TOK_DEV, QW // BLK, BLK)
    live = block_index >= 0
    safe = jnp.maximum(block_index, 0)
    owner = (jnp.arange(BLOCKS, dtype=jnp.int32) // CAP)[:, None]
    rows = owner * row_blocks + safe // col_blocks
    cols = jnp.arange(N_TENSOR, dtype=jnp.int32)[None, :] * col_blocks + safe % col_blocks

    def one_block(item):
        row, col, alive = item
        left = lax.dynamic_index_in_dim(inputs4, row, axis=2, keepdims=False).astype(jnp.float32)
        right = lax.dynamic_index_in_dim(grads4, col, axis=2, keepdims=False).astype(jnp.float32)
        part = jnp.einsum('ptd,pte->pde', left, right)
        part = lax.optimization_barrier(part.astype(jnp.bfloat16)).astype(jnp.float32)
        return jnp.where(alive, lax.optimization_barrier(jnp.sum(part, axis=0)), jnp.zeros((BLK, BLK), jnp.float32))
    flat = lax.map(one_block, (rows.reshape(-1).astype(jnp.int32), cols.reshape(-1).astype(jnp.int32), live.reshape(-1)))
    block_grads = flat.reshape(BLOCKS, N_TENSOR, BLK, BLK)
    return (block_grads, input_grad)
```

```python
import functools
import math

import jax
import jax.numpy as jnp
from jax import lax
from jax.experimental import pallas as pl
from jax.experimental.pallas import tpu as pltpu
from jax.sharding import PartitionSpec as P

MESH = pl.DeviceIdType.MESH
F32 = jnp.float32
BF16 = jnp.bfloat16
TOK = 384
D = 8192
BLK = 128
CAP = 6
COLS = 1024
HALF = 512
OWN_COLS = 2048
BROWS = CAP * BLK
TOKENS = 12288
QW = 4096
U_OF_K = (0, -1, 1, 2)


class Payload:
    def __init__(self, env, buf, sems):
        self.env = env
        self.buf = buf
        self.rows = buf.shape[2]
        self.send, self.recv, self.sib_send, self.sib_recv = sems

    def off(self, lane, du, dv):
        return (du, dv) if lane == 0 else (dv, du)

    def piece(self, core, dx, dy, lane, q0, nq):
        quarter = self.rows // 4
        return self.buf.at[self.env.chip(dx, dy), core, pl.ds((lane * 2 + q0) * quarter, nq * quarter), :]

    def copy(self, lane, du, dv, q0, nq, axis, sign, event):
        dx, dy = self.off(lane, du, dv)
        ref = self.piece(self.env.core, dx, dy, lane, q0, nq)
        step = self.off(lane, sign, 0) if axis == 0 else self.off(lane, 0, sign)
        return pltpu.make_async_remote_copy(
            src_ref=ref,
            dst_ref=ref,
            send_sem=self.send.at[lane, event],
            recv_sem=self.recv.at[lane, event],
            device_id=self.env.peer(*step),
            device_id_type=MESH,
        )

    def put(self, *args):
        c = self.copy(*args)
        c.start()
        self.env.started.append(c)

    def got(self, lane, du, dv, q0, nq, event):
        self.copy(lane, du, dv, q0, nq, 0, 1, event).wait_recv()

    def sib_copy(self, core, lane, dx, dy):
        ref = self.piece(core, dx, dy, lane, 0, 2)
        at = lane * 16 + (dx % 4) * 4 + dy % 4
        return pltpu.make_async_remote_copy(
            src_ref=ref,
            dst_ref=ref,
            send_sem=self.sib_send.at[at],
            recv_sem=self.sib_recv.at[at],
            device_id=self.env.sibling,
            device_id_type=MESH,
        )

    def to_sibling(self, lane, du, dv):
        c = self.sib_copy(self.env.core, lane, *self.off(lane, du, dv))
        c.start()
        self.env.started.append(c)

    def from_sibling(self, dx, dy):
        for lane in (0, 1):
            self.sib_copy(1 - self.env.core, lane, dx, dy).wait_recv()

    def own(self):
        for lane in (0, 1):
            for axis, base in ((0, 0), (1, 4)):
                self.put(lane, 0, 0, 0, 2, axis, 1, base)
                self.put(lane, 0, 0, 0, 2, axis, -1, base + 1)
        for lane in (0, 1):
            self.to_sibling(lane, 0, 0)

    def u1(self, lane):
        for k, du, sign, event in ((1, -1, 1, 0), (2, 1, -1, 1)):
            self.got(lane, du, 0, 0, 2, event)
            self.put(lane, du, 0, event, 1, 0, sign, 2 + event)
            self.put(lane, du, 0, 0, 2, 1, 1, 4 + 4 * k)
            self.put(lane, du, 0, 0, 2, 1, -1, 5 + 4 * k)
            self.to_sibling(lane, du, 0)

    def u2(self, lane):
        self.got(lane, 2, 0, 0, 1, 2)
        self.got(lane, 2, 0, 1, 1, 3)
        self.put(lane, 2, 0, 0, 2, 1, 1, 16)
        self.put(lane, 2, 0, 0, 2, 1, -1, 17)
        self.to_sibling(lane, 2, 0)

    def v1(self, lane, k):
        du = U_OF_K[k]
        for dv, sign, event in ((-1, 1, 0), (1, -1, 1)):
            self.got(lane, du, dv, 0, 2, 4 + 4 * k + event)
            self.put(lane, du, dv, event, 1, 1, sign, 6 + 4 * k + event)
            self.to_sibling(lane, du, dv)

    def v2(self, lane, k):
        du = U_OF_K[k]
        self.got(lane, du, 2, 0, 1, 6 + 4 * k)
        self.got(lane, du, 2, 1, 1, 7 + 4 * k)
        self.to_sibling(lane, du, 2)

    def events(self):
        both = lambda f, *a: [functools.partial(f, 0, *a), functools.partial(f, 1, *a)]
        seq = []
        seq += both(self.u1) + both(self.v1, 0)
        seq += both(self.u2)
        seq += both(self.v1, 1) + both(self.v1, 2)
        seq += both(self.v2, 0) + both(self.v1, 3)
        seq += both(self.v2, 1) + both(self.v2, 2) + both(self.v2, 3)
        return seq


DONE_AFTER = {
    3: ((-1, 0), (1, 0), (0, -1), (0, 1)),
    9: ((-1, -1), (-1, 1), (1, -1), (1, 1)),
    11: ((2, 0), (0, 2)),
    17: ((2, -1), (2, 1), (-1, 2), (1, 2)),
    19: ((2, 2),),
}
CHIP_ORDER = ((0, 0),) + DONE_AFTER[3] + DONE_AFTER[9] + DONE_AFTER[11] + DONE_AFTER[17] + DONE_AFTER[19]
GRAD_ORDER = (
    (2, 2), (2, 1), (2, -1), (1, 2), (-1, 2), (2, 0), (0, 2), (1, 1),
    (1, -1), (-1, 1), (-1, -1), (1, 0), (-1, 0), (0, 1), (0, -1), (0, 0),
)


class Env:
    pass


def rel(dx, dy):
    return (dx % 4) * 4 + dy % 4


def kernel(
    x_hbm, w_hbm, b_hbm, i_hbm, gout, iout,
    xv, wv, bv, fv, idxv, idxs, acc_t, acc_s, few, slab, dv, gt, dense, pv, ss, sr, rv1, rv2, ru1, ru2, sqv, wcol, iacc,
    loc_sem, p_send, p_recv, p_sib_send, p_sib_recv,
    i_send, i_recv, f_send, f_recv, d_send, d_recv, q_send, q_recv, g_send, g_recv, r_send, r_recv,
):
    dp = lax.axis_index("dp")
    z = lax.axis_index("tensor")
    core = lax.rem(dp, 2)
    x = lax.rem(dp // 2, 4)
    y = dp // 8
    env = Env()
    env.core = core
    env.started = []

    def mod4(a, d):
        return a if d == 0 else lax.rem(a + (d % 4), 4)

    env.chip = lambda dx, dy: mod4(y, dy) * 4 + mod4(x, dx)
    env.peer = lambda dx, dy: (env.chip(dx, dy) * 2 + core, z)
    env.sibling = (env.chip(0, 0) * 2 + 1 - core, z)
    zpeer = lambda d: (dp, mod4(z, d))

    def remote(src, dst, send, recv, device):
        return pltpu.make_async_remote_copy(
            src_ref=src, dst_ref=dst, send_sem=send, recv_sem=recv, device_id=device, device_id_type=MESH
        )

    def go(c):
        c.start()
        env.started.append(c)

    here = env.chip(0, 0)
    own_b = pltpu.make_async_copy(b_hbm, bv.at[here, core], loc_sem.at[0])
    own_i = pltpu.make_async_copy(i_hbm, idxv.at[core, y, x, z], loc_sem.at[1])
    own_w = [
        pltpu.make_async_copy(w_hbm.at[:, pl.ds(HALF * h, HALF)], wv.at[h, here, core], loc_sem.at[2 + h])
        for h in (0, 1)
    ]
    own_x = pltpu.make_async_copy(x_hbm, xv, loc_sem.at[4])
    own_b.start()
    own_i.start()
    for c in own_w:
        c.start()
    own_x.start()

    barrier = pltpu.get_barrier_semaphore()
    peers = [env.sibling]
    peers += [env.peer(d, 0) for d in (1, 2, 3)] + [env.peer(0, d) for d in (1, 2, 3)] + [zpeer(d) for d in (1, 2, 3)]
    for p in peers:
        pl.semaphore_signal(barrier, inc=1, device_id=p, device_id_type=MESH)
    pl.semaphore_wait(barrier, len(peers))

    blocks, teach0, teach1 = [
        Payload(env, buf, (p_send.at[n], p_recv.at[n], p_sib_send.at[n], p_sib_recv.at[n]))
        for n, buf in ((0, bv), (1, wv.at[0]), (2, wv.at[1]))
    ]
    teach = (teach0, teach1)

    own_i.wait()
    own_b.wait()

    def idx_copies(stage):
        if stage == 0:
            ref = idxv.at[core, y, x, z]
            return [remote(ref, ref, i_send.at[d - 1], i_recv.at[d - 1], zpeer(d)) for d in (1, 2, 3)]
        if stage == 1:
            ref = idxv.at[core, y, x]
            return [remote(ref, ref, i_send.at[2 + d], i_recv.at[2 + d], env.peer(d, 0)) for d in (1, 2, 3)]
        if stage == 2:
            ref = idxv.at[core, y]
            return [remote(ref, ref, i_send.at[5 + d], i_recv.at[5 + d], env.peer(0, d)) for d in (1, 2, 3)]
        ref = idxv.at[core]
        return [remote(ref, ref, i_send.at[9], i_recv.at[9], env.sibling)]

    def idx_start(stage):
        for c in idx_copies(stage):
            go(c)

    def idx_wait(stage):
        for n in range(3 if stage < 3 else 1):
            d = n + 1
            if stage == 0:
                ref = idxv.at[core, y, x, mod4(z, -d)]
            elif stage == 1:
                ref = idxv.at[core, y, mod4(x, -d)]
            elif stage == 2:
                ref = idxv.at[core, mod4(y, -d)]
            else:
                ref = idxv.at[1 - core]
            at = 3 * stage + n
            remote(ref, ref, i_send.at[at], i_recv.at[at], env.sibling).wait_recv()

    idx_start(0)
    blocks.own()
    own_w[0].wait()
    teach0.own()
    idx_wait(0)
    idx_start(1)
    own_w[1].wait()
    own_x.wait()
    acc_t[...] = jnp.zeros_like(acc_t)
    acc_s[...] = jnp.zeros_like(acc_s)
    ev = blocks.events()
    for n, f in enumerate(ev):
        f()
        if n == 1:
            idx_wait(1)
            idx_start(2)
        if n == 5:
            idx_wait(2)
            idx_start(3)
        if n == 9:
            idx_wait(3)
            to_smem = pltpu.make_async_copy(idxv, idxs, loc_sem.at[5])
            to_smem.start()
            to_smem.wait()

    def f_copy(d, half):
        src = bv.at[pl.ds(mod4(z, d) * 4 + half * 2, 2), core]
        dst = fv.at[3 - d, pl.ds(half * 2, 2), core]
        at = (d - 1) * 2 + half
        return remote(src, dst, f_send.at[at], f_recv.at[at], zpeer(d))

    for d in (1, 3, 2):
        for half in (0, 1):
            go(f_copy(d, half))

    def f_sib(r, core_of):
        ref = fv.at[r, :, core_of]
        return remote(ref, ref, f_send.at[6 + r], f_recv.at[6 + r], env.sibling)

    def f_arrived(d):
        for half in (0, 1):
            f_copy(d, half).wait_recv()
        go(f_sib(3 - d, core))

    for dx, dy in CHIP_ORDER:
        blocks.from_sibling(dx, dy)

    for cc in (0, 1):
        few[cc, CAP] = jnp.zeros((BLK, BLK), BF16)
        dense[cc, 16] = jnp.zeros((BLK, BLK), BF16)

    def build(src, places):
        for cc in (0, 1):
            few[cc, 0:CAP] = src(cc).reshape(CAP, BLK, BLK)
            for q in range(16):
                slab[cc * 256 + q // 8 * BLK:cc * 256 + (q // 8 + 1) * BLK, q % 8 * BLK:(q % 8 + 1) * BLK] = few[
                    cc, places(cc, 8 + q)
                ]

    def columns_of(chip):
        return pl.ds(pl.multiple_of(chip * 512, 512), 512)

    def student(n):
        chip = n
        cy, cx = n // 4, n % 4
        build(
            lambda cc: bv[chip, cc],
            lambda cc, lane: idxs[cc, cy, cx, z, 0, lane],
        )
        for h in (0, 1):
            for t in (0, 1):
                acc_s[h, :, t * 256:(t + 1) * 256] += jnp.dot(
                    xv[:, chip * 512:(chip + 1) * 512],
                    slab[:, h * HALF + t * 256:h * HALF + (t + 1) * 256],
                    preferred_element_type=F32,
                )

    def teacher(h, dx, dy):
        teach[h].from_sibling(dx, dy)
        chip = env.chip(dx, dy)
        cols = columns_of(chip)
        for t in (0, 1):
            acc_t[h, :, t * 256:(t + 1) * 256] += jnp.dot(
                xv[:, cols],
                wv[h, chip, :, :, t * 256:(t + 1) * 256].reshape(512, 256),
                preferred_element_type=F32,
            )

    def d_copy(h, dist, event):
        rows = ((0, TOK), (0, TOK), (0, TOK // 2), (TOK // 2, TOK // 2))[event]
        ref = dv.at[h, mod4(z, dist), pl.ds(*rows), :]
        return remote(ref, ref, d_send.at[h, event], d_recv.at[h, event], zpeer(1 if event in (0, 2) else -1))

    def finish_half(h):
        t = acc_t[h]
        s = t * t
        s = s[:, 0:128] + s[:, 128:256] + s[:, 256:384] + s[:, 384:512]
        if h == 0:
            wcol[...] = s
        else:
            wcol[...] += s
        diff = acc_s[h] - t
        acc_s[h] = diff
        dv[h, z] = diff.astype(BF16)
        go(d_copy(h, 0, 0))
        go(d_copy(h, 0, 1))

    def d_forward(h):
        d_copy(h, -1, 0).wait_recv()
        go(d_copy(h, -1, 2))
        d_copy(h, 1, 1).wait_recv()
        go(d_copy(h, 1, 3))

    def d_last(h):
        d_copy(h, 2, 2).wait_recv()
        d_copy(h, 2, 3).wait_recv()

    def input_grad(n, dist, halves, first):
        plane = mod4(z, dist)
        if dist == 0:
            src = lambda cc: bv[z * 4 + n, cc]
        else:
            src = lambda cc: fv[dist - 1, n, cc]
        build(src, lambda cc, lane: idxs[cc, z, n, plane, 0, lane])
        for t in (0, 1):
            at = slice(n * 512 + t * 256, n * 512 + (t + 1) * 256)
            total = None
            for h in halves:
                term = lax.dot_general(
                    dv[h, plane],
                    slab[t * 256:(t + 1) * 256, h * HALF:(h + 1) * HALF],
                    (((1,), (1,)), ((), ())),
                    preferred_element_type=F32,
                )
                total = term if total is None else total + term
            if first:
                iacc[:, at] = total
            else:
                iacc[:, at] += total

    teach1.own()
    tasks = [functools.partial(student, n) for n in range(16)]
    tasks.append(functools.partial(teacher, 0, 0, 0))

    def run(count):
        for _ in range(count):
            if tasks:
                tasks.pop(0)()

    for n, f in enumerate(teach0.events()):
        f()
        tasks += [functools.partial(teacher, 0, *c) for c in DONE_AFTER.get(n, ())]
        run(1)
    for d in (1, 3, 2):
        tasks.append(functools.partial(f_arrived, d))
    tasks.append(functools.partial(finish_half, 0))
    tasks.append(functools.partial(teacher, 1, 0, 0))
    tail = []
    for n, f in enumerate(teach1.events()):
        f()
        tasks += [functools.partial(teacher, 1, *c) for c in DONE_AFTER.get(n, ())]
        run(2)
        if n == 15:
            d_forward(0)
    run(len(tasks))
    finish_half(1)

    row = jnp.sum(jnp.transpose(wcol[...]), axis=0, keepdims=True)
    sqv[0] = jnp.broadcast_to(row, (8, TOK))

    def q_copy(d):
        return remote(sqv.at[0], sqv.at[d], q_send.at[d - 1], q_recv.at[d - 1], zpeer(d))

    for d in (1, 2, 3):
        go(q_copy(d))
    d_last(0)
    for r in range(3):
        f_sib(r, 1 - core).wait_recv()
    for d in (1, 2, 3):
        q_copy(d).wait_recv()
    squares = sqv[0] + sqv[1] + sqv[2] + sqv[3]
    weight = 1.0 / (squares / QW + 1e-05)
    scale = 1.0 / math.sqrt(TOKENS)
    wcol[...] = jnp.transpose(jnp.broadcast_to(weight[0:1], (128, TOK)))
    for h in (0, 1):
        for t in range(4):
            g = wcol[...] * acc_s[h, :, t * 128:(t + 1) * 128] * scale
            gt[h * HALF + t * 128:h * HALF + (t + 1) * 128, :] = jnp.transpose(g).astype(BF16)

    def s_copy(dx, dy):
        at = rel(dx, dy)
        return remote(ss.at[at], sr.at[at], g_send.at[at], g_recv.at[at], env.sibling)

    def grads(dx, dy):
        chip = env.chip(dx, dy)
        cx, cy = mod4(x, dx), mod4(y, dy)
        for cc in (0, 1):
            full = jnp.dot(
                gt[...],
                xv[:, pl.ds(pl.multiple_of(chip * 512 + cc * 256, 256), 256)],
                preferred_element_type=F32,
            ).astype(BF16)
            for q in range(16):
                dense[cc, q] = full[q % 8 * BLK:(q % 8 + 1) * BLK, q // 8 * BLK:(q // 8 + 1) * BLK]
        for out, cc in ((ss, 1 - core), (pv, core)):
            for s in range(CAP):
                out[rel(dx, dy), s * BLK:(s + 1) * BLK, :] = dense[cc, idxs[cc, cy, cx, z, 0, s]]
        go(s_copy(dx, dy))

    def merge(dx, dy):
        s_copy(dx, dy).wait_recv()
        at = rel(dx, dy)
        pv[at] = (pv[at].astype(F32) + sr[at].astype(F32)).astype(BF16)

    def lane_off(lane, du, dv_):
        return (du, dv_) if lane == 0 else (dv_, du)

    def rows_of(lane, q0, nq):
        return pl.ds((lane * 2 + q0) * 192, nq * 192)

    def hop(lane, axis, sign):
        return env.peer(*lane_off(lane, sign, 0)) if axis == 0 else env.peer(*lane_off(lane, 0, sign))

    def v1_copy(lane, k, side):
        at = rel(*lane_off(lane, U_OF_K[k], 2))
        n = lane * 16 + k * 4 + side
        return remote(
            pv.at[at, rows_of(lane, side, 1), :], rv1.at[lane, k, side], r_send.at[n], r_recv.at[n],
            hop(lane, 1, 1 - 2 * side),
        )

    def v2_copy(lane, k, side):
        at = rel(*lane_off(lane, U_OF_K[k], 1 - 2 * side))
        n = lane * 16 + k * 4 + 2 + side
        return remote(
            pv.at[at, rows_of(lane, 0, 2), :], rv2.at[lane, k, side], r_send.at[n], r_recv.at[n],
            hop(lane, 1, 1 - 2 * side),
        )

    def u1_copy(lane, side):
        at = rel(*lane_off(lane, 2, 0))
        n = 32 + lane * 4 + side
        return remote(
            pv.at[at, rows_of(lane, side, 1), :], ru1.at[lane, side], r_send.at[n], r_recv.at[n],
            hop(lane, 0, 1 - 2 * side),
        )

    def u2_copy(lane, side):
        at = rel(*lane_off(lane, 1 - 2 * side, 0))
        n = 32 + lane * 4 + 2 + side
        return remote(
            pv.at[at, rows_of(lane, 0, 2), :], ru2.at[lane, side], r_send.at[n], r_recv.at[n],
            hop(lane, 0, 1 - 2 * side),
        )

    def add(at, lane, q0, nq, got):
        rows = rows_of(lane, q0, nq)
        pv[at, rows, :] = (pv[at, rows, :].astype(F32) + got.astype(F32)).astype(BF16)

    def rv_first(lane, k):
        for side in (0, 1):
            go(v1_copy(lane, k, side))

    def rv_second(lane, k):
        for side in (0, 1):
            v1_copy(lane, k, side).wait_recv()
            add(rel(*lane_off(lane, U_OF_K[k], 1 - 2 * side)), lane, side, 1, rv1[lane, k, side])
            go(v2_copy(lane, k, side))

    def rv_third(lane, k):
        for side in (0, 1):
            v2_copy(lane, k, side).wait_recv()
        at = rel(*lane_off(lane, U_OF_K[k], 0))
        add(at, lane, 0, 2, rv2[lane, k, 0].astype(F32) + rv2[lane, k, 1].astype(F32))

    def ru_first(lane):
        for side in (0, 1):
            go(u1_copy(lane, side))

    def ru_second(lane):
        for side in (0, 1):
            u1_copy(lane, side).wait_recv()
            add(rel(*lane_off(lane, 1 - 2 * side, 0)), lane, side, 1, ru1[lane, side])
            go(u2_copy(lane, side))

    def ru_third(lane):
        for side in (0, 1):
            u2_copy(lane, side).wait_recv()
        total = pv[0, rows_of(lane, 0, 2), :].astype(F32) + ru2[lane, 0].astype(F32) + ru2[lane, 1].astype(F32)
        for s in range(3):
            gout[lane * 3 + s, 0] = jnp.transpose(total[s * BLK:(s + 1) * BLK])

    lanes = lambda f, *a: [functools.partial(f, 0, *a), functools.partial(f, 1, *a)]
    after = {
        0: lanes(rv_first, 3),
        4: lanes(rv_first, 2) + lanes(rv_first, 1),
        6: lanes(rv_second, 3) + lanes(rv_first, 0),
        8: [],
        10: lanes(rv_second, 2) + lanes(rv_second, 1) + lanes(rv_third, 3) + lanes(ru_first),
        12: [],
        14: lanes(rv_second, 0) + lanes(rv_third, 2) + lanes(rv_third, 1) + lanes(ru_second),
    }
    for n, c in enumerate(GRAD_ORDER):
        grads(*c)
        if n > 0:
            merge(*GRAD_ORDER[n - 1])
            for f in after.get(n - 1, ()):
                f()
        if n == 6:
            d_forward(1)
    merge(*GRAD_ORDER[15])

    for n in range(4):
        input_grad(n, 0, (0, 1), True)
    for f in lanes(rv_third, 0):
        f()
    for n in range(4):
        input_grad(n, 1, (0, 1), False)
        input_grad(n, 3, (0, 1), False)
    d_last(1)
    for n in range(4):
        input_grad(n, 2, (0, 1), False)
    for n in range(16):
        at = slice(n * 128, (n + 1) * 128)
        iout[:, at] = (iacc[:, at] * (wcol[...] * scale)).astype(BF16)
    for f in lanes(ru_third):
        f()
    for c in env.started:
        c.wait_send()


def body(hidden_states, teacher_weight, student_blocks, block_index):
    listed = block_index[:, 0]
    slot = jnp.arange(16, dtype=jnp.int32)
    hit = listed[:, None] == slot[None, :]
    order = jnp.arange(CAP, dtype=jnp.int32)
    pick = jnp.min(jnp.where(hit, order[:, None], CAP), axis=0).astype(jnp.int32)
    places = jnp.concatenate(
        [jnp.where(listed < 0, 16, listed), jnp.zeros((2,), jnp.int32), pick, jnp.zeros((104,), jnp.int32)]
    ).reshape(1, 128)
    any_spec = pl.BlockSpec(memory_space=pl.ANY)
    vmem_spec = pl.BlockSpec(memory_space=pltpu.VMEM)
    dma = pltpu.SemaphoreType.DMA
    block_grads, input_grad = pl.pallas_call(
        kernel,
        out_shape=(
            jax.ShapeDtypeStruct((CAP, 1, BLK, BLK), F32),
            jax.ShapeDtypeStruct((TOK, OWN_COLS), BF16),
        ),
        in_specs=[any_spec] * 4,
        out_specs=(vmem_spec, vmem_spec),
        scratch_shapes=[
            pltpu.VMEM((TOK, D), BF16),
            pltpu.VMEM((2, 16, 2, 256, HALF), BF16),
            pltpu.VMEM((16, 2, BROWS, BLK), BF16),
            pltpu.VMEM((3, 4, 2, BROWS, BLK), BF16),
            pltpu.VMEM((2, 4, 4, 4, 1, 128), jnp.int32),
            pltpu.SMEM((2, 4, 4, 4, 1, 128), jnp.int32),
            pltpu.VMEM((2, TOK, HALF), F32),
            pltpu.VMEM((2, TOK, HALF), F32),
            pltpu.VMEM((2, CAP + 1, BLK, BLK), BF16),
            pltpu.VMEM((512, COLS), BF16),
            pltpu.VMEM((2, 4, TOK, HALF), BF16),
            pltpu.VMEM((COLS, TOK), BF16),
            pltpu.VMEM((2, 17, BLK, BLK), BF16),
            pltpu.VMEM((16, BROWS, BLK), BF16),
            pltpu.VMEM((16, BROWS, BLK), BF16),
            pltpu.VMEM((16, BROWS, BLK), BF16),
            pltpu.VMEM((2, 4, 2, 192, BLK), BF16),
            pltpu.VMEM((2, 4, 2, 384, BLK), BF16),
            pltpu.VMEM((2, 2, 192, BLK), BF16),
            pltpu.VMEM((2, 2, 384, BLK), BF16),
            pltpu.VMEM((4, 8, TOK), F32),
            pltpu.VMEM((TOK, 128), F32),
            pltpu.VMEM((TOK, OWN_COLS), F32),
            dma((6,)),
            dma((3, 2, 20)),
            dma((3, 2, 20)),
            dma((3, 32)),
            dma((3, 32)),
            dma((10,)),
            dma((10,)),
            dma((9,)),
            dma((9,)),
            dma((2, 4)),
            dma((2, 4)),
            dma((3,)),
            dma((3,)),
            dma((16,)),
            dma((16,)),
            dma((40,)),
            dma((40,)),
        ],
        compiler_params=pltpu.CompilerParams(
            collective_id=0, has_side_effects=True, vmem_limit_bytes=63 * 1024 * 1024
        ),
        cost_estimate=pl.CostEstimate(flops=26 * 10**9, bytes_accessed=10 * 10**6, transcendentals=0),
    )(hidden_states, teacher_weight, student_blocks.reshape(BROWS, BLK), places)
    return block_grads, input_grad


def solution(mesh):
    in_specs = (P("dp", None), P("dp", "tensor"), P("dp", "tensor", None, None), P("dp", "tensor"))
    out_specs = (P("dp", "tensor", None, None), P("dp", "tensor"))
    return jax.shard_map(body, mesh=mesh, in_specs=in_specs, out_specs=out_specs, check_vma=False)
```

```python
import functools
import math

import jax
import jax.numpy as jnp
from jax import lax
from jax.experimental import pallas as pl
from jax.experimental.pallas import tpu as pltpu
from jax.sharding import PartitionSpec as P

MESH = pl.DeviceIdType.MESH
F32 = jnp.float32
BF16 = jnp.bfloat16
TOK = 384
D = 8192
BLK = 128
CAP = 6
COLS = 1024
HALF = 512
OWN_COLS = 2048
BROWS = CAP * BLK
TOKENS = 12288
QW = 4096
U_OF_K = (0, -1, 1, 2)
LAG0 = 6
LAG1 = 26
OWN0 = 0
OWN1 = 18
START = 6
ARRIVED = 32
FORWARD = 40
FILL = 4
RUN0 = 1
RUN1 = 3


class Payload:
    def __init__(self, env, buf, sems):
        self.env = env
        self.buf = buf
        self.rows = buf.shape[2]
        self.send, self.recv, self.sib_send, self.sib_recv = sems
        self.on_piece = None
        self.started = []

    def off(self, lane, du, dv):
        return (du, dv) if lane == 0 else (dv, du)

    def piece(self, core, dx, dy, lane, q0, nq):
        quarter = self.rows // 4
        return self.buf.at[self.env.chip(dx, dy), core, pl.ds((lane * 2 + q0) * quarter, nq * quarter), :]

    def copy(self, lane, du, dv, q0, nq, axis, sign, event):
        dx, dy = self.off(lane, du, dv)
        ref = self.piece(self.env.core, dx, dy, lane, q0, nq)
        step = self.off(lane, sign, 0) if axis == 0 else self.off(lane, 0, sign)
        return pltpu.make_async_remote_copy(
            src_ref=ref,
            dst_ref=ref,
            send_sem=self.send.at[lane, event],
            recv_sem=self.recv.at[lane, event],
            device_id=self.env.peer(*step),
            device_id_type=MESH,
        )

    def put(self, *args):
        c = self.copy(*args)
        c.start()
        self.started.append(c)

    def got(self, lane, du, dv, q0, nq, event):
        self.copy(lane, du, dv, q0, nq, 0, 1, event).wait_recv()

    def sib_copy(self, core, lane, dx, dy):
        ref = self.piece(core, dx, dy, lane, 0, 2)
        at = lane * 16 + (dx % 4) * 4 + dy % 4
        return pltpu.make_async_remote_copy(
            src_ref=ref,
            dst_ref=ref,
            send_sem=self.sib_send.at[at],
            recv_sem=self.sib_recv.at[at],
            device_id=self.env.sibling,
            device_id_type=MESH,
        )

    def to_sibling(self, lane, du, dv):
        c = self.sib_copy(self.env.core, lane, *self.off(lane, du, dv))
        c.start()
        self.started.append(c)
        if self.on_piece is not None:
            self.on_piece(lane, *self.off(lane, du, dv))

    def sent(self):
        for c in self.started:
            c.wait_send()
        self.started.clear()

    def from_sibling(self, dx, dy):
        for lane in (0, 1):
            self.sib_copy(1 - self.env.core, lane, dx, dy).wait_recv()

    def own(self):
        for lane in (0, 1):
            for axis, base in ((0, 0), (1, 4)):
                self.put(lane, 0, 0, 0, 2, axis, 1, base)
                self.put(lane, 0, 0, 0, 2, axis, -1, base + 1)
        for lane in (0, 1):
            self.to_sibling(lane, 0, 0)

    def u1(self, lane):
        for k, du, sign, event in ((1, -1, 1, 0), (2, 1, -1, 1)):
            self.got(lane, du, 0, 0, 2, event)
            self.put(lane, du, 0, event, 1, 0, sign, 2 + event)
            self.put(lane, du, 0, 0, 2, 1, 1, 4 + 4 * k)
            self.put(lane, du, 0, 0, 2, 1, -1, 5 + 4 * k)
            self.to_sibling(lane, du, 0)

    def u2(self, lane):
        self.got(lane, 2, 0, 0, 1, 2)
        self.got(lane, 2, 0, 1, 1, 3)
        self.put(lane, 2, 0, 0, 2, 1, 1, 16)
        self.put(lane, 2, 0, 0, 2, 1, -1, 17)
        self.to_sibling(lane, 2, 0)

    def v1(self, lane, k):
        du = U_OF_K[k]
        for dv, sign, event in ((-1, 1, 0), (1, -1, 1)):
            self.got(lane, du, dv, 0, 2, 4 + 4 * k + event)
            self.put(lane, du, dv, event, 1, 1, sign, 6 + 4 * k + event)
            self.to_sibling(lane, du, dv)

    def v2(self, lane, k):
        du = U_OF_K[k]
        self.got(lane, du, 2, 0, 1, 6 + 4 * k)
        self.got(lane, du, 2, 1, 1, 7 + 4 * k)
        self.to_sibling(lane, du, 2)

    def events(self):
        both = lambda f, *a: [functools.partial(f, 0, *a), functools.partial(f, 1, *a)]
        seq = []
        seq += both(self.u1) + both(self.v1, 0)
        seq += both(self.u2)
        seq += both(self.v1, 1) + both(self.v1, 2)
        seq += both(self.v2, 0) + both(self.v1, 3)
        seq += both(self.v2, 1) + both(self.v2, 2) + both(self.v2, 3)
        return seq


DONE_AFTER = {
    3: ((-1, 0), (1, 0), (0, -1), (0, 1)),
    9: ((-1, -1), (-1, 1), (1, -1), (1, 1)),
    11: ((2, 0), (0, 2)),
    17: ((2, -1), (2, 1), (-1, 2), (1, 2)),
    19: ((2, 2),),
}
CHIP_ORDER = ((0, 0),) + DONE_AFTER[3] + DONE_AFTER[9] + DONE_AFTER[11] + DONE_AFTER[17] + DONE_AFTER[19]
GRAD_ORDER = (
    (2, 2), (2, 1), (2, -1), (1, 2), (-1, 2), (2, 0), (0, 2), (1, 1),
    (1, -1), (-1, 1), (-1, -1), (1, 0), (-1, 0), (0, 1), (0, -1), (0, 0),
)


class Env:
    pass


def rel(dx, dy):
    return (dx % 4) * 4 + dy % 4


def kernel(
    x_hbm, w_hbm, b_hbm, i_smem, gout, iout,
    xv, wv, bv, fv, idxv, idxs, acc_t, acc_s, few, slab, dv, gt, dense, sr, rv1, rv2, ru1, ru2, sqv, wcol, iacc,
    loc_sem, p_send, p_recv, p_sib_send, p_sib_recv,
    i_send, i_recv, f_send, f_recv, fs_send, fs_recv, d_send, d_recv, q_send, q_recv, g_send, g_recv, r_send, r_recv,
):
    dp = lax.axis_index("dp")
    z = lax.axis_index("tensor")
    core = lax.rem(dp, 2)
    x = lax.rem(dp // 2, 4)
    y = dp // 8
    env = Env()
    env.core = core
    env.started = []

    def mod4(a, d):
        return a if d == 0 else lax.rem(a + (d % 4), 4)

    env.chip = lambda dx, dy: mod4(y, dy) * 4 + mod4(x, dx)
    env.peer = lambda dx, dy: (env.chip(dx, dy) * 2 + core, z)
    env.sibling = (env.chip(0, 0) * 2 + 1 - core, z)
    zpeer = lambda d: (dp, mod4(z, d))

    def remote(src, dst, send, recv, device):
        return pltpu.make_async_remote_copy(
            src_ref=src, dst_ref=dst, send_sem=send, recv_sem=recv, device_id=device, device_id_type=MESH
        )

    def go(c):
        c.start()
        env.started.append(c)

    here = env.chip(0, 0)
    own_b = pltpu.make_async_copy(b_hbm, bv.at[here, core], loc_sem.at[0])
    own_w = [
        pltpu.make_async_copy(w_hbm.at[:, pl.ds(HALF * h, HALF)], wv.at[h, here, core], loc_sem.at[2 + h])
        for h in (0, 1)
    ]
    own_x = pltpu.make_async_copy(x_hbm, xv, loc_sem.at[4])
    own_b.start()
    for c in own_w:
        c.start()
    own_x.start()

    barrier = pltpu.get_barrier_semaphore()
    peers = [env.sibling]
    peers += [env.peer(d, 0) for d in (1, 2, 3)] + [env.peer(0, d) for d in (1, 2, 3)] + [zpeer(d) for d in (1, 2, 3)]
    for p in peers:
        pl.semaphore_signal(barrier, inc=1, device_id=p, device_id_type=MESH)
    pl.semaphore_wait(barrier, len(peers))

    blocks, teach0, teach1 = [
        Payload(env, buf, (p_send.at[n], p_recv.at[n], p_sib_send.at[n], p_sib_recv.at[n]))
        for n, buf in ((0, bv), (1, wv.at[0]), (2, wv.at[1]))
    ]
    teach = (teach0, teach1)

    lane_of = lax.broadcasted_iota(jnp.int32, (1, 128), 1)
    row = jnp.full((1, 128), CAP, jnp.int32)
    for s in range(CAP):
        place = jnp.full((1, 128), i_smem[s, 0], jnp.int32)
        row = jnp.where(lane_of == place + 8, s, row)
    for s in range(CAP):
        place = jnp.full((1, 128), i_smem[s, 0], jnp.int32)
        row = jnp.where(lane_of == s, jnp.where(place < 0, 16, place), row)
    idxv[core, y, x, z] = row
    own_b.wait()

    def idx_copies(stage):
        if stage == 0:
            ref = idxv.at[core, y, x, z]
            return [remote(ref, ref, i_send.at[d - 1], i_recv.at[d - 1], zpeer(d)) for d in (1, 2, 3)]
        if stage == 1:
            ref = idxv.at[core, y, x]
            return [remote(ref, ref, i_send.at[2 + d], i_recv.at[2 + d], env.peer(d, 0)) for d in (1, 2, 3)]
        if stage == 2:
            ref = idxv.at[core, y]
            return [remote(ref, ref, i_send.at[5 + d], i_recv.at[5 + d], env.peer(0, d)) for d in (1, 2, 3)]
        ref = idxv.at[core]
        return [remote(ref, ref, i_send.at[9], i_recv.at[9], env.sibling)]

    def idx_start(stage):
        for c in idx_copies(stage):
            go(c)

    def idx_wait(stage):
        for n in range(3 if stage < 3 else 1):
            d = n + 1
            if stage == 0:
                ref = idxv.at[core, y, x, mod4(z, -d)]
            elif stage == 1:
                ref = idxv.at[core, y, mod4(x, -d)]
            elif stage == 2:
                ref = idxv.at[core, mod4(y, -d)]
            else:
                ref = idxv.at[1 - core]
            at = 3 * stage + n
            remote(ref, ref, i_send.at[at], i_recv.at[at], env.sibling).wait_recv()

    def f_piece(lane, dx, dy):
        cx, cy = mod4(x, dx), mod4(y, dy)
        r = lax.rem(z - cy + 4, 4) - 1
        rows = pl.ds(lane * (BROWS // 2), BROWS // 2)
        return remote(
            bv.at[cy * 4 + cx, core, rows, :], fv.at[r, cx, core, rows, :],
            f_send.at[lane, rel(dx, dy)], f_recv.at[lane, r * 4 + cx], (dp, cy),
        )

    def f_start(lane, dx, dy):
        @pl.when(mod4(y, dy) != z)
        def _():
            f_piece(lane, dx, dy).start()

    def f_sent():
        for lane in (0, 1):
            for dx in range(4):
                for dy in range(4):
                    @pl.when(mod4(y, dy) != z)
                    def _():
                        f_piece(lane, dx, dy).wait_send()

    def f_sib(r, core_of):
        ref = fv.at[r, :, core_of]
        return remote(ref, ref, fs_send.at[r], fs_recv.at[r], env.sibling)

    def f_arrived(r):
        for cx in range(4):
            for lane in (0, 1):
                ref = fv.at[r, cx, core, pl.ds(lane * (BROWS // 2), BROWS // 2), :]
                remote(ref, ref, fs_send.at[r], f_recv.at[lane, r * 4 + cx], env.sibling).wait_recv()
        go(f_sib(r, core))

    blocks.on_piece = f_start

    def build(src, places, slots, store):
        for cc in (0, 1):
            few[cc, 0:CAP] = src(cc).reshape(CAP, BLK, BLK)
            for q in slots:
                store(cc, q // 8, q % 8, few[cc, places(cc, 8 + q)])

    def columns_of(chip):
        return pl.ds(pl.multiple_of(chip * 512, 512), 512)

    def student(dx, dy):
        blocks.from_sibling(dx, dy)
        chip = env.chip(dx, dy)
        cx, cy = mod4(x, dx), mod4(y, dy)
        cols = columns_of(chip)

        def store(cc, row, col, val):
            slab[cc * 256 + row * BLK:cc * 256 + (row + 1) * BLK, col * BLK:(col + 1) * BLK] = val

        build(lambda cc: bv[chip, cc], lambda cc, lane: idxs[cc, cy, cx, z, 0, lane], range(16), store)
        for h in (0, 1):
            for t in (0, 1):
                acc_s[h, :, t * 256:(t + 1) * 256] += jnp.dot(
                    xv[:, cols],
                    slab[:, h * HALF + t * 256:h * HALF + (t + 1) * 256],
                    preferred_element_type=F32,
                )

    def teacher(h, dx, dy):
        teach[h].from_sibling(dx, dy)
        chip = env.chip(dx, dy)
        cols = columns_of(chip)
        for t in (0, 1):
            acc_t[h, :, t * 256:(t + 1) * 256] += jnp.dot(
                xv[:, cols],
                wv[h, chip, :, :, t * 256:(t + 1) * 256].reshape(512, 256),
                preferred_element_type=F32,
            )

    def d_copy(h, dist, event):
        rows = ((0, TOK), (0, TOK), (0, TOK // 2), (TOK // 2, TOK // 2))[event]
        ref = dv.at[h, mod4(z, dist), pl.ds(*rows), :]
        return remote(ref, ref, d_send.at[h, event], d_recv.at[h, event], zpeer(1 if event in (0, 2) else -1))

    def finish_half(h):
        t = acc_t[h]
        s = t * t
        s = s[:, 0:128] + s[:, 128:256] + s[:, 256:384] + s[:, 384:512]
        if h == 0:
            wcol[...] = s
        else:
            wcol[...] += s
        diff = acc_s[h] - t
        acc_s[h] = diff
        dv[h, z] = diff.astype(BF16)

    def d_start(h):
        go(d_copy(h, 0, 0))
        go(d_copy(h, 0, 1))

    def d_forward(h):
        d_copy(h, -1, 0).wait_recv()
        go(d_copy(h, -1, 2))
        d_copy(h, 1, 1).wait_recv()
        go(d_copy(h, 1, 3))

    def d_last(h):
        d_copy(h, 2, 2).wait_recv()
        d_copy(h, 2, 3).wait_recv()

    def slab_of(n, dist, h, store):
        plane = mod4(z, dist)
        src = (lambda cc: bv[z * 4 + n, cc]) if dist == 0 else (lambda cc: fv[dist - 1, n, cc])
        slots = [q for q in range(16) if q % 8 // 4 == h]
        build(src, lambda cc, lane: idxs[cc, z, n, plane, 0, lane], slots, store)

    def grad_term(n, dist, h, cut, first):
        for t in (0, 1):
            at = slice(n * 512 + t * 256, n * 512 + (t + 1) * 256)
            term = lax.dot_general(
                dv[h, mod4(z, dist)], cut(t), (((1,), (1,)), ((), ())), preferred_element_type=F32
            )
            if first:
                iacc[:, at] = term
            else:
                iacc[:, at] += term

    def grad_first(n, dist):
        def store(cc, row, col, val):
            slab[cc * 256 + row * BLK:cc * 256 + (row + 1) * BLK, col * BLK:(col + 1) * BLK] = val

        slab_of(n, dist, 0, store)
        grad_term(n, dist, 0, lambda t: slab[t * 256:(t + 1) * 256, 0:HALF], dist == 0)

    def prebuild(n, dist):
        def store(cc, row, col, val):
            wv[0, dist * 4 + n, cc, row * BLK:(row + 1) * BLK, (col - 4) * BLK:(col - 3) * BLK] = val

        slab_of(n, dist, 1, store)

    def grad_second(n, dist):
        grad_term(n, dist, 1, lambda t: wv[0, dist * 4 + n, t], False)

    tasks, later = [], []

    def run(count, pos):
        for _ in range(count):
            if tasks:
                tasks.pop(0)()
            elif later and later[0][0] <= pos:
                later.pop(0)[1]()

    def ready():
        idx_wait(3)
        to_smem = pltpu.make_async_copy(idxv, idxs, loc_sem.at[5])
        to_smem.start()
        own_x.wait()
        acc_t[...] = jnp.zeros_like(acc_t)
        acc_s[...] = jnp.zeros_like(acc_s)
        for cc in (0, 1):
            few[cc, CAP] = jnp.zeros((BLK, BLK), BF16)
            dense[cc, 16] = jnp.zeros((BLK, BLK), BF16)
        to_smem.wait()

    def idx_step(stage):
        idx_wait(stage - 1)
        idx_start(stage)

    def second_own():
        own_w[1].wait()
        teach1.own()

    def f_here():
        for r in range(3):
            f_sib(r, 1 - core).wait_recv()

    call = functools.partial

    state = {"half": False, "forward": False}

    def forward():
        if state["half"] and not state["forward"]:
            state["forward"] = True
            d_forward(0)

    def half_done():
        finish_half(0)
        d_start(0)
        state["half"] = True
        later.extend((0, call(grad_first, n, 0)) for n in range(4))
        later.append((0, teach0.sent))
        later.extend((0, call(prebuild, n, 0)) for n in range(4))
        later.extend((ARRIVED, call(f_arrived, r)) for r in (0, 2, 1))
        later.append((ARRIVED, f_here))
        later.extend((ARRIVED, call(prebuild, n, dist)) for dist in (1, 3, 2) for n in range(4))
        later.append((FORWARD, forward))
        later.extend((FORWARD, call(grad_first, n, dist)) for dist in (1, 3) for n in range(4))
        later.append((99, call(d_last, 0)))
        later.extend((99, call(grad_first, n, 2)) for n in range(4))

    idx_start(0)
    blocks.own()
    own_w[0].wait()
    merged = [(OWN0, 0, teach0.own), (OWN1, 0, second_own)]
    merged += [(at, 1, call(idx_step, stage)) for stage, at in ((1, 1), (2, 3), (3, 5))]
    merged.append((START, 1, call(tasks.append, ready)))
    merged.append((START, 2, call(tasks.append, call(student, 0, 0))))
    merged.append((START, 3, call(tasks.append, call(teacher, 0, 0, 0))))
    for n, f in enumerate(blocks.events()):
        merged.append((n, 4, f))
        merged += [(max(n, START), 5, call(tasks.append, call(student, *c))) for c in DONE_AFTER.get(n, ())]
    for h, at in ((0, LAG0), (1, LAG1)):
        for n, f in enumerate(teach[h].events()):
            merged.append((at + n, 6 + 2 * h, f))
            merged += [
                (max(at + n, START), 7 + 2 * h, call(tasks.append, call(teacher, h, *c))) for c in DONE_AFTER.get(n, ())
            ]
    merged.append((LAG0 + 19, 8, call(tasks.append, half_done)))
    merged.append((LAG0 + 19, 8, call(tasks.append, call(teacher, 1, 0, 0))))
    merged.append((FORWARD, 9, forward))
    merged.sort(key=lambda e: e[:2])
    for at, kind, f in merged:
        f()
        if at >= START and kind in (4, 6, 8):
            run(RUN0 if at < LAG0 + 20 else RUN1, at)
    while tasks:
        run(1, 0)
    finish_half(1)

    row = jnp.sum(jnp.transpose(wcol[...]), axis=0, keepdims=True)
    sqv[0] = jnp.broadcast_to(row, (8, TOK))

    def q_copy(d):
        return remote(sqv.at[0], sqv.at[d], q_send.at[d - 1], q_recv.at[d - 1], zpeer(d))

    for d in (1, 2, 3):
        go(q_copy(d))
    run(FILL, 99)
    for d in (1, 2, 3):
        q_copy(d).wait_recv()
    d_start(1)
    squares = sqv[0] + sqv[1] + sqv[2] + sqv[3]
    weight = 1.0 / (squares / QW + 1e-05)
    scale = 1.0 / math.sqrt(TOKENS)
    wcol[...] = jnp.transpose(jnp.broadcast_to(weight[0:1], (128, TOK)))
    for h in (0, 1):
        for t in range(4):
            g = wcol[...] * acc_s[h, :, t * 128:(t + 1) * 128] * scale
            gt[h * HALF + t * 128:h * HALF + (t + 1) * 128, :] = jnp.transpose(g).astype(BF16)

    run(len(later), 99)
    blocks.sent()
    f_sent()
    ss, pv = bv.at[:, 0], bv.at[:, 1]

    def s_copy(dx, dy):
        at = rel(dx, dy)
        return remote(ss.at[at], sr.at[at], g_send.at[at], g_recv.at[at], env.sibling)

    def grads(dx, dy):
        chip = env.chip(dx, dy)
        cx, cy = mod4(x, dx), mod4(y, dy)
        for cc in (0, 1):
            full = jnp.dot(
                gt[...],
                xv[:, pl.ds(pl.multiple_of(chip * 512 + cc * 256, 256), 256)],
                preferred_element_type=F32,
            ).astype(BF16)
            for q in range(16):
                dense[cc, q] = full[q % 8 * BLK:(q % 8 + 1) * BLK, q // 8 * BLK:(q // 8 + 1) * BLK]
        for out, cc in ((ss, 1 - core), (pv, core)):
            for s in range(CAP):
                out[rel(dx, dy), s * BLK:(s + 1) * BLK, :] = dense[cc, idxs[cc, cy, cx, z, 0, s]]
        go(s_copy(dx, dy))

    def merge(dx, dy):
        s_copy(dx, dy).wait_recv()
        at = rel(dx, dy)
        pv[at] = (pv[at].astype(F32) + sr[at].astype(F32)).astype(BF16)

    def lane_off(lane, du, dv_):
        return (du, dv_) if lane == 0 else (dv_, du)

    def rows_of(lane, q0, nq):
        return pl.ds((lane * 2 + q0) * 192, nq * 192)

    def hop(lane, axis, sign):
        return env.peer(*lane_off(lane, sign, 0)) if axis == 0 else env.peer(*lane_off(lane, 0, sign))

    def v1_copy(lane, k, side):
        at = rel(*lane_off(lane, U_OF_K[k], 2))
        n = lane * 16 + k * 4 + side
        return remote(
            pv.at[at, rows_of(lane, side, 1), :], rv1.at[lane, k, side], r_send.at[n], r_recv.at[n],
            hop(lane, 1, 1 - 2 * side),
        )

    def v2_copy(lane, k, side):
        at = rel(*lane_off(lane, U_OF_K[k], 1 - 2 * side))
        n = lane * 16 + k * 4 + 2 + side
        return remote(
            pv.at[at, rows_of(lane, 0, 2), :], rv2.at[lane, k, side], r_send.at[n], r_recv.at[n],
            hop(lane, 1, 1 - 2 * side),
        )

    def u1_copy(lane, side):
        at = rel(*lane_off(lane, 2, 0))
        n = 32 + lane * 4 + side
        return remote(
            pv.at[at, rows_of(lane, side, 1), :], ru1.at[lane, side], r_send.at[n], r_recv.at[n],
            hop(lane, 0, 1 - 2 * side),
        )

    def u2_copy(lane, side):
        at = rel(*lane_off(lane, 1 - 2 * side, 0))
        n = 32 + lane * 4 + 2 + side
        return remote(
            pv.at[at, rows_of(lane, 0, 2), :], ru2.at[lane, side], r_send.at[n], r_recv.at[n],
            hop(lane, 0, 1 - 2 * side),
        )

    def add(at, lane, q0, nq, got):
        rows = rows_of(lane, q0, nq)
        pv[at, rows, :] = (pv[at, rows, :].astype(F32) + got.astype(F32)).astype(BF16)

    def rv_first(lane, k):
        for side in (0, 1):
            go(v1_copy(lane, k, side))

    def rv_second(lane, k):
        for side in (0, 1):
            v1_copy(lane, k, side).wait_recv()
            add(rel(*lane_off(lane, U_OF_K[k], 1 - 2 * side)), lane, side, 1, rv1[lane, k, side])
            go(v2_copy(lane, k, side))

    def rv_third(lane, k):
        for side in (0, 1):
            v2_copy(lane, k, side).wait_recv()
        at = rel(*lane_off(lane, U_OF_K[k], 0))
        add(at, lane, 0, 2, rv2[lane, k, 0].astype(F32) + rv2[lane, k, 1].astype(F32))

    def ru_first(lane):
        for side in (0, 1):
            go(u1_copy(lane, side))

    def ru_second(lane):
        for side in (0, 1):
            u1_copy(lane, side).wait_recv()
            add(rel(*lane_off(lane, 1 - 2 * side, 0)), lane, side, 1, ru1[lane, side])
            go(u2_copy(lane, side))

    def ru_third(lane):
        for side in (0, 1):
            u2_copy(lane, side).wait_recv()
        total = pv[0, rows_of(lane, 0, 2), :].astype(F32) + ru2[lane, 0].astype(F32) + ru2[lane, 1].astype(F32)
        for s in range(3):
            gout[lane * 3 + s, 0] = jnp.transpose(total[s * BLK:(s + 1) * BLK])

    lanes = lambda f, *a: [functools.partial(f, 0, *a), functools.partial(f, 1, *a)]
    after = {
        0: lanes(rv_first, 3),
        4: lanes(rv_first, 2) + lanes(rv_first, 1),
        6: lanes(rv_second, 3) + lanes(rv_first, 0),
        8: [],
        10: lanes(rv_second, 2) + lanes(rv_second, 1) + lanes(rv_third, 3) + lanes(ru_first),
        12: [],
        14: lanes(rv_second, 0) + lanes(rv_third, 2) + lanes(rv_third, 1) + lanes(ru_second),
    }
    for n, c in enumerate(GRAD_ORDER):
        grads(*c)
        if n > 0:
            merge(*GRAD_ORDER[n - 1])
            for f in after.get(n - 1, ()):
                f()
        if n == 10:
            d_forward(1)
    merge(*GRAD_ORDER[15])

    for n in range(4):
        grad_second(n, 0)
    for f in lanes(rv_third, 0):
        f()
    for n in range(4):
        grad_second(n, 1)
        grad_second(n, 3)
    d_last(1)
    for n in range(4):
        grad_second(n, 2)
    for n in range(16):
        at = slice(n * 128, (n + 1) * 128)
        iout[:, at] = (iacc[:, at] * (wcol[...] * scale)).astype(BF16)
    for f in lanes(ru_third):
        f()
    for c in env.started:
        c.wait_send()
    teach1.sent()


def body(hidden_states, teacher_weight, student_blocks, block_index):
    any_spec = pl.BlockSpec(memory_space=pl.ANY)
    vmem_spec = pl.BlockSpec(memory_space=pltpu.VMEM)
    dma = pltpu.SemaphoreType.DMA
    block_grads, input_grad = pl.pallas_call(
        kernel,
        out_shape=(
            jax.ShapeDtypeStruct((CAP, 1, BLK, BLK), F32),
            jax.ShapeDtypeStruct((TOK, OWN_COLS), BF16),
        ),
        in_specs=[any_spec] * 3 + [pl.BlockSpec(memory_space=pltpu.SMEM)],
        out_specs=(vmem_spec, vmem_spec),
        scratch_shapes=[
            pltpu.VMEM((TOK, D), BF16),
            pltpu.VMEM((2, 16, 2, 256, HALF), BF16),
            pltpu.VMEM((16, 2, BROWS, BLK), BF16),
            pltpu.VMEM((3, 4, 2, BROWS, BLK), BF16),
            pltpu.VMEM((2, 4, 4, 4, 1, 128), jnp.int32),
            pltpu.SMEM((2, 4, 4, 4, 1, 128), jnp.int32),
            pltpu.VMEM((2, TOK, HALF), F32),
            pltpu.VMEM((2, TOK, HALF), F32),
            pltpu.VMEM((2, CAP + 1, BLK, BLK), BF16),
            pltpu.VMEM((512, COLS), BF16),
            pltpu.VMEM((2, 4, TOK, HALF), BF16),
            pltpu.VMEM((COLS, TOK), BF16),
            pltpu.VMEM((2, 17, BLK, BLK), BF16),
            pltpu.VMEM((16, BROWS, BLK), BF16),
            pltpu.VMEM((2, 4, 2, 192, BLK), BF16),
            pltpu.VMEM((2, 4, 2, 384, BLK), BF16),
            pltpu.VMEM((2, 2, 192, BLK), BF16),
            pltpu.VMEM((2, 2, 384, BLK), BF16),
            pltpu.VMEM((4, 8, TOK), F32),
            pltpu.VMEM((TOK, 128), F32),
            pltpu.VMEM((TOK, OWN_COLS), F32),
            dma((6,)),
            dma((3, 2, 20)),
            dma((3, 2, 20)),
            dma((3, 32)),
            dma((3, 32)),
            dma((10,)),
            dma((10,)),
            dma((2, 16)),
            dma((2, 12)),
            dma((3,)),
            dma((3,)),
            dma((2, 4)),
            dma((2, 4)),
            dma((3,)),
            dma((3,)),
            dma((16,)),
            dma((16,)),
            dma((40,)),
            dma((40,)),
        ],
        compiler_params=pltpu.CompilerParams(
            collective_id=0, has_side_effects=True, vmem_limit_bytes=63 * 1024 * 1024
        ),
        cost_estimate=pl.CostEstimate(flops=26 * 10**9, bytes_accessed=10 * 10**6, transcendentals=0),
    )(hidden_states, teacher_weight, student_blocks.reshape(BROWS, BLK), block_index)
    return block_grads, input_grad


def solution(mesh):
    in_specs = (P("dp", None), P("dp", "tensor"), P("dp", "tensor", None, None), P("dp", "tensor"))
    out_specs = (P("dp", "tensor", None, None), P("dp", "tensor"))
    return jax.shard_map(body, mesh=mesh, in_specs=in_specs, out_specs=out_specs, check_vma=False)
```

```python
import functools
import math

import jax
import jax.numpy as jnp
from jax import lax
from jax.experimental import pallas as pl
from jax.experimental.pallas import tpu as pltpu
from jax.sharding import PartitionSpec as P

MESH = pl.DeviceIdType.MESH
F32 = jnp.float32
BF16 = jnp.bfloat16
TOK = 384
D = 8192
BLK = 128
CAP = 6
COLS = 1024
HALF = 512
OWN_COLS = 2048
BROWS = CAP * BLK
TOKENS = 12288
QW = 4096
U_OF_K = (0, -1, 1, 2)
LAG0 = 6
LAG1 = 26
OWN0 = 0
OWN1 = 18
START = 6
ARRIVED = 32
FORWARD = 40
FILL = 4
RUN0 = 1
RUN1 = 3


class Payload:
    def __init__(self, env, buf, sems):
        self.env = env
        self.buf = buf
        self.rows = buf.shape[2]
        self.send, self.recv, self.sib_send, self.sib_recv = sems
        self.on_piece = None
        self.started = []

    def off(self, lane, du, dv):
        return (du, dv) if lane == 0 else (dv, du)

    def piece(self, core, dx, dy, lane, q0, nq):
        quarter = self.rows // 4
        return self.buf.at[self.env.chip(dx, dy), core, pl.ds((lane * 2 + q0) * quarter, nq * quarter), :]

    def copy(self, lane, du, dv, q0, nq, axis, sign, event):
        dx, dy = self.off(lane, du, dv)
        ref = self.piece(self.env.core, dx, dy, lane, q0, nq)
        step = self.off(lane, sign, 0) if axis == 0 else self.off(lane, 0, sign)
        return pltpu.make_async_remote_copy(
            src_ref=ref,
            dst_ref=ref,
            send_sem=self.send.at[lane, event],
            recv_sem=self.recv.at[lane, event],
            device_id=self.env.peer(*step),
            device_id_type=MESH,
        )

    def put(self, *args):
        c = self.copy(*args)
        c.start()
        self.started.append(c)

    def got(self, lane, du, dv, q0, nq, event):
        self.copy(lane, du, dv, q0, nq, 0, 1, event).wait_recv()

    def sib_copy(self, core, lane, dx, dy):
        ref = self.piece(core, dx, dy, lane, 0, 2)
        at = lane * 16 + (dx % 4) * 4 + dy % 4
        return pltpu.make_async_remote_copy(
            src_ref=ref,
            dst_ref=ref,
            send_sem=self.sib_send.at[at],
            recv_sem=self.sib_recv.at[at],
            device_id=self.env.sibling,
            device_id_type=MESH,
        )

    def to_sibling(self, lane, du, dv):
        c = self.sib_copy(self.env.core, lane, *self.off(lane, du, dv))
        c.start()
        self.started.append(c)
        if self.on_piece is not None:
            self.on_piece(lane, *self.off(lane, du, dv))

    def sent(self):
        for c in self.started:
            c.wait_send()
        self.started.clear()

    def from_sibling(self, dx, dy):
        for lane in (0, 1):
            self.sib_copy(1 - self.env.core, lane, dx, dy).wait_recv()

    def own(self):
        for lane in (0, 1):
            for axis, base in ((0, 0), (1, 4)):
                self.put(lane, 0, 0, 0, 2, axis, 1, base)
                self.put(lane, 0, 0, 0, 2, axis, -1, base + 1)
        for lane in (0, 1):
            self.to_sibling(lane, 0, 0)

    def u1(self, lane):
        for k, du, sign, event in ((1, -1, 1, 0), (2, 1, -1, 1)):
            self.got(lane, du, 0, 0, 2, event)
            self.put(lane, du, 0, event, 1, 0, sign, 2 + event)
            self.put(lane, du, 0, 0, 2, 1, 1, 4 + 4 * k)
            self.put(lane, du, 0, 0, 2, 1, -1, 5 + 4 * k)
            self.to_sibling(lane, du, 0)

    def u2(self, lane):
        self.got(lane, 2, 0, 0, 1, 2)
        self.got(lane, 2, 0, 1, 1, 3)
        self.put(lane, 2, 0, 0, 2, 1, 1, 16)
        self.put(lane, 2, 0, 0, 2, 1, -1, 17)
        self.to_sibling(lane, 2, 0)

    def v1(self, lane, k):
        du = U_OF_K[k]
        for dv, sign, event in ((-1, 1, 0), (1, -1, 1)):
            self.got(lane, du, dv, 0, 2, 4 + 4 * k + event)
            self.put(lane, du, dv, event, 1, 1, sign, 6 + 4 * k + event)
            self.to_sibling(lane, du, dv)

    def v2(self, lane, k):
        du = U_OF_K[k]
        self.got(lane, du, 2, 0, 1, 6 + 4 * k)
        self.got(lane, du, 2, 1, 1, 7 + 4 * k)
        self.to_sibling(lane, du, 2)

    def events(self):
        both = lambda f, *a: [functools.partial(f, 0, *a), functools.partial(f, 1, *a)]
        seq = []
        seq += both(self.u1) + both(self.v1, 0)
        seq += both(self.u2)
        seq += both(self.v1, 1) + both(self.v1, 2)
        seq += both(self.v2, 0) + both(self.v1, 3)
        seq += both(self.v2, 1) + both(self.v2, 2) + both(self.v2, 3)
        return seq


DONE_AFTER = {
    3: ((-1, 0), (1, 0), (0, -1), (0, 1)),
    9: ((-1, -1), (-1, 1), (1, -1), (1, 1)),
    11: ((2, 0), (0, 2)),
    17: ((2, -1), (2, 1), (-1, 2), (1, 2)),
    19: ((2, 2),),
}
CHIP_ORDER = ((0, 0),) + DONE_AFTER[3] + DONE_AFTER[9] + DONE_AFTER[11] + DONE_AFTER[17] + DONE_AFTER[19]
GRAD_ORDER = (
    (2, 2), (2, 1), (2, -1), (1, 2), (-1, 2), (2, 0), (0, 2), (1, 1),
    (1, -1), (-1, 1), (-1, -1), (1, 0), (-1, 0), (0, 1), (0, -1), (0, 0),
)


class Env:
    pass


def rel(dx, dy):
    return (dx % 4) * 4 + dy % 4


def kernel(
    x_hbm, w_hbm, b_hbm, i_smem, gout, iout,
    xv, wv, bv, fv, idxv, idxs, acc_t, acc_s, few, slab, dv, gt, dense, sr, rv1, rv2, ru1, ru2, sqv, wcol, iacc,
    loc_sem, p_send, p_recv, p_sib_send, p_sib_recv,
    i_send, i_recv, f_send, f_recv, fs_send, fs_recv, d_send, d_recv, q_send, q_recv, g_send, g_recv, r_send, r_recv,
):
    dp = lax.axis_index("dp")
    z = lax.axis_index("tensor")
    core = lax.rem(dp, 2)
    x = lax.rem(dp // 2, 4)
    y = dp // 8
    env = Env()
    env.core = core
    env.started = []

    def mod4(a, d):
        return a if d == 0 else lax.rem(a + (d % 4), 4)

    env.chip = lambda dx, dy: mod4(y, dy) * 4 + mod4(x, dx)
    env.peer = lambda dx, dy: (env.chip(dx, dy) * 2 + core, z)
    env.sibling = (env.chip(0, 0) * 2 + 1 - core, z)
    zpeer = lambda d: (dp, mod4(z, d))

    def remote(src, dst, send, recv, device):
        return pltpu.make_async_remote_copy(
            src_ref=src, dst_ref=dst, send_sem=send, recv_sem=recv, device_id=device, device_id_type=MESH
        )

    def go(c):
        c.start()
        env.started.append(c)

    here = env.chip(0, 0)
    own_b = pltpu.make_async_copy(b_hbm, bv.at[here, core], loc_sem.at[0])
    own_w = [
        pltpu.make_async_copy(w_hbm.at[:, pl.ds(HALF * h, HALF)], wv.at[h, here, core], loc_sem.at[2 + h])
        for h in (0, 1)
    ]
    own_x = pltpu.make_async_copy(x_hbm, xv, loc_sem.at[4])
    own_b.start()
    for c in own_w:
        c.start()
    own_x.start()

    barrier = pltpu.get_barrier_semaphore()
    peers = [env.sibling]
    peers += [env.peer(d, 0) for d in (1, 2, 3)] + [env.peer(0, d) for d in (1, 2, 3)] + [zpeer(d) for d in (1, 2, 3)]
    for p in peers:
        pl.semaphore_signal(barrier, inc=1, device_id=p, device_id_type=MESH)
    pl.semaphore_wait(barrier, len(peers))

    blocks, teach0, teach1 = [
        Payload(env, buf, (p_send.at[n], p_recv.at[n], p_sib_send.at[n], p_sib_recv.at[n]))
        for n, buf in ((0, bv), (1, wv.at[0]), (2, wv.at[1]))
    ]
    teach = (teach0, teach1)

    lane_of = lax.broadcasted_iota(jnp.int32, (1, 128), 1)
    row = jnp.full((1, 128), CAP, jnp.int32)
    for s in range(CAP):
        place = jnp.full((1, 128), i_smem[0, s], jnp.int32)
        row = jnp.where(lane_of == place + 8, s, row)
    for s in range(CAP):
        place = jnp.full((1, 128), i_smem[0, s], jnp.int32)
        row = jnp.where(lane_of == s, jnp.where(place < 0, 16, place), row)
    idxv[core, y, x, z] = row
    own_b.wait()

    def idx_copies(stage):
        if stage == 0:
            ref = idxv.at[core, y, x, z]
            return [remote(ref, ref, i_send.at[d - 1], i_recv.at[d - 1], zpeer(d)) for d in (1, 2, 3)]
        if stage == 1:
            ref = idxv.at[core, y, x]
            return [remote(ref, ref, i_send.at[2 + d], i_recv.at[2 + d], env.peer(d, 0)) for d in (1, 2, 3)]
        if stage == 2:
            ref = idxv.at[core, y]
            return [remote(ref, ref, i_send.at[5 + d], i_recv.at[5 + d], env.peer(0, d)) for d in (1, 2, 3)]
        ref = idxv.at[core]
        return [remote(ref, ref, i_send.at[9], i_recv.at[9], env.sibling)]

    def idx_start(stage):
        for c in idx_copies(stage):
            go(c)

    def idx_wait(stage):
        for n in range(3 if stage < 3 else 1):
            d = n + 1
            if stage == 0:
                ref = idxv.at[core, y, x, mod4(z, -d)]
            elif stage == 1:
                ref = idxv.at[core, y, mod4(x, -d)]
            elif stage == 2:
                ref = idxv.at[core, mod4(y, -d)]
            else:
                ref = idxv.at[1 - core]
            at = 3 * stage + n
            remote(ref, ref, i_send.at[at], i_recv.at[at], env.sibling).wait_recv()

    def f_piece(lane, dx, dy):
        cx, cy = mod4(x, dx), mod4(y, dy)
        r = lax.rem(z - cy + 4, 4) - 1
        rows = pl.ds(lane * (BROWS // 2), BROWS // 2)
        return remote(
            bv.at[cy * 4 + cx, core, rows, :], fv.at[r, cx, core, rows, :],
            f_send.at[lane, rel(dx, dy)], f_recv.at[lane, r * 4 + cx], (dp, cy),
        )

    def f_start(lane, dx, dy):
        @pl.when(mod4(y, dy) != z)
        def _():
            f_piece(lane, dx, dy).start()

    def f_sent():
        for lane in (0, 1):
            for dx in range(4):
                for dy in range(4):
                    @pl.when(mod4(y, dy) != z)
                    def _():
                        f_piece(lane, dx, dy).wait_send()

    def f_sib(r, core_of):
        ref = fv.at[r, :, core_of]
        return remote(ref, ref, fs_send.at[r], fs_recv.at[r], env.sibling)

    def f_arrived(r):
        for cx in range(4):
            for lane in (0, 1):
                ref = fv.at[r, cx, core, pl.ds(lane * (BROWS // 2), BROWS // 2), :]
                remote(ref, ref, fs_send.at[r], f_recv.at[lane, r * 4 + cx], env.sibling).wait_recv()
        go(f_sib(r, core))

    blocks.on_piece = f_start

    def build(src, places, slots, store):
        for cc in (0, 1):
            few[cc, 0:CAP] = src(cc).reshape(CAP, BLK, BLK)
            for q in slots:
                store(cc, q // 8, q % 8, few[cc, places(cc, 8 + q)])

    def columns_of(chip):
        return pl.ds(pl.multiple_of(chip * 512, 512), 512)

    def student(dx, dy):
        blocks.from_sibling(dx, dy)
        chip = env.chip(dx, dy)
        cx, cy = mod4(x, dx), mod4(y, dy)
        cols = columns_of(chip)

        def store(cc, row, col, val):
            slab[cc * 256 + row * BLK:cc * 256 + (row + 1) * BLK, col * BLK:(col + 1) * BLK] = val

        build(lambda cc: bv[chip, cc], lambda cc, lane: idxs[cc, cy, cx, z, 0, lane], range(16), store)
        for h in (0, 1):
            for t in (0, 1):
                acc_s[h, :, t * 256:(t + 1) * 256] += jnp.dot(
                    xv[:, cols],
                    slab[:, h * HALF + t * 256:h * HALF + (t + 1) * 256],
                    preferred_element_type=F32,
                )

    def teacher(h, dx, dy):
        teach[h].from_sibling(dx, dy)
        chip = env.chip(dx, dy)
        cols = columns_of(chip)
        for t in (0, 1):
            acc_t[h, :, t * 256:(t + 1) * 256] += jnp.dot(
                xv[:, cols],
                wv[h, chip, :, :, t * 256:(t + 1) * 256].reshape(512, 256),
                preferred_element_type=F32,
            )

    def d_copy(h, dist, event):
        rows = ((0, TOK), (0, TOK), (0, TOK // 2), (TOK // 2, TOK // 2))[event]
        ref = dv.at[h, mod4(z, dist), pl.ds(*rows), :]
        return remote(ref, ref, d_send.at[h, event], d_recv.at[h, event], zpeer(1 if event in (0, 2) else -1))

    def finish_half(h):
        t = acc_t[h]
        s = t * t
        s = s[:, 0:128] + s[:, 128:256] + s[:, 256:384] + s[:, 384:512]
        if h == 0:
            wcol[...] = s
        else:
            wcol[...] += s
        diff = acc_s[h] - t
        acc_s[h] = diff
        dv[h, z] = diff.astype(BF16)

    def d_start(h):
        go(d_copy(h, 0, 0))
        go(d_copy(h, 0, 1))

    def d_forward(h):
        d_copy(h, -1, 0).wait_recv()
        go(d_copy(h, -1, 2))
        d_copy(h, 1, 1).wait_recv()
        go(d_copy(h, 1, 3))

    def d_last(h):
        d_copy(h, 2, 2).wait_recv()
        d_copy(h, 2, 3).wait_recv()

    def slab_of(n, dist, h, store):
        plane = mod4(z, dist)
        src = (lambda cc: bv[z * 4 + n, cc]) if dist == 0 else (lambda cc: fv[dist - 1, n, cc])
        slots = [q for q in range(16) if q % 8 // 4 == h]
        build(src, lambda cc, lane: idxs[cc, z, n, plane, 0, lane], slots, store)

    def grad_term(n, dist, h, cut, first):
        for t in (0, 1):
            at = slice(n * 512 + t * 256, n * 512 + (t + 1) * 256)
            term = lax.dot_general(
                dv[h, mod4(z, dist)], cut(t), (((1,), (1,)), ((), ())), preferred_element_type=F32
            )
            if first:
                iacc[:, at] = term
            else:
                iacc[:, at] += term

    def grad_first(n, dist):
        def store(cc, row, col, val):
            slab[cc * 256 + row * BLK:cc * 256 + (row + 1) * BLK, col * BLK:(col + 1) * BLK] = val

        slab_of(n, dist, 0, store)
        grad_term(n, dist, 0, lambda t: slab[t * 256:(t + 1) * 256, 0:HALF], dist == 0)

    def prebuild(n, dist):
        def store(cc, row, col, val):
            wv[0, dist * 4 + n, cc, row * BLK:(row + 1) * BLK, (col - 4) * BLK:(col - 3) * BLK] = val

        slab_of(n, dist, 1, store)

    def prebuild_all(dist):
        def step(n, carry):
            prebuild(n, dist)
            return carry

        lax.fori_loop(0, 4, step, 0)

    def grad_second(n, dist):
        grad_term(n, dist, 1, lambda t: wv[0, dist * 4 + n, t], False)

    tasks, later = [], []

    def run(count, pos):
        for _ in range(count):
            if tasks:
                tasks.pop(0)()
            elif later and later[0][0] <= pos:
                later.pop(0)[1]()

    def ready():
        idx_wait(3)
        to_smem = pltpu.make_async_copy(idxv, idxs, loc_sem.at[5])
        to_smem.start()
        own_x.wait()
        acc_t[...] = jnp.zeros_like(acc_t)
        acc_s[...] = jnp.zeros_like(acc_s)
        for cc in (0, 1):
            few[cc, CAP] = jnp.zeros((BLK, BLK), BF16)
            dense[cc, 16] = jnp.zeros((BLK, BLK), BF16)
        to_smem.wait()

    def idx_step(stage):
        idx_wait(stage - 1)
        idx_start(stage)

    def second_own():
        own_w[1].wait()
        teach1.own()

    def f_here():
        for r in range(3):
            f_sib(r, 1 - core).wait_recv()

    call = functools.partial

    state = {"half": False, "forward": False}

    def forward():
        if state["half"] and not state["forward"]:
            state["forward"] = True
            d_forward(0)

    def half_done():
        finish_half(0)
        d_start(0)
        state["half"] = True
        later.extend((0, call(grad_first, n, 0)) for n in range(4))
        later.append((0, teach0.sent))
        later.append((0, call(prebuild_all, 0)))
        later.extend((ARRIVED, call(f_arrived, r)) for r in (0, 2, 1))
        later.append((ARRIVED, f_here))
        later.extend((ARRIVED, call(prebuild_all, dist)) for dist in (1, 3, 2))
        later.append((FORWARD, forward))
        later.extend((FORWARD, call(grad_first, n, dist)) for dist in (1, 3) for n in range(4))
        later.append((99, call(d_last, 0)))
        later.extend((99, call(grad_first, n, 2)) for n in range(4))

    idx_start(0)
    blocks.own()
    own_w[0].wait()
    merged = [(OWN0, 0, teach0.own), (OWN1, 0, second_own)]
    merged += [(at, 1, call(idx_step, stage)) for stage, at in ((1, 1), (2, 3), (3, 5))]
    merged.append((START, 1, call(tasks.append, ready)))
    merged.append((START, 2, call(tasks.append, call(student, 0, 0))))
    merged.append((START, 3, call(tasks.append, call(teacher, 0, 0, 0))))
    for n, f in enumerate(blocks.events()):
        merged.append((n, 4, f))
        merged += [(max(n, START), 5, call(tasks.append, call(student, *c))) for c in DONE_AFTER.get(n, ())]
    for h, at in ((0, LAG0), (1, LAG1)):
        for n, f in enumerate(teach[h].events()):
            merged.append((at + n, 6 + 2 * h, f))
            merged += [
                (max(at + n, START), 7 + 2 * h, call(tasks.append, call(teacher, h, *c))) for c in DONE_AFTER.get(n, ())
            ]
    merged.append((LAG0 + 19, 8, call(tasks.append, half_done)))
    merged.append((LAG0 + 19, 8, call(tasks.append, call(teacher, 1, 0, 0))))
    merged.append((FORWARD, 9, forward))
    merged.sort(key=lambda e: e[:2])
    for at, kind, f in merged:
        f()
        if at >= START and kind in (4, 6, 8):
            run(RUN0 if at < LAG0 + 20 else RUN1, at)
    while tasks:
        run(1, 0)
    finish_half(1)

    row = jnp.sum(jnp.transpose(wcol[...]), axis=0, keepdims=True)
    sqv[0] = jnp.broadcast_to(row, (8, TOK))

    def q_copy(d):
        return remote(sqv.at[0], sqv.at[d], q_send.at[d - 1], q_recv.at[d - 1], zpeer(d))

    for d in (1, 2, 3):
        go(q_copy(d))
    run(FILL, 99)
    for d in (1, 2, 3):
        q_copy(d).wait_recv()
    d_start(1)
    squares = sqv[0] + sqv[1] + sqv[2] + sqv[3]
    weight = 1.0 / (squares / QW + 1e-05)
    scale = 1.0 / math.sqrt(TOKENS)
    wcol[...] = jnp.transpose(jnp.broadcast_to(weight[0:1], (128, TOK)))
    for h in (0, 1):
        for t in range(4):
            g = wcol[...] * acc_s[h, :, t * 128:(t + 1) * 128] * scale
            gt[h * HALF + t * 128:h * HALF + (t + 1) * 128, :] = jnp.transpose(g).astype(BF16)

    run(len(later), 99)
    blocks.sent()
    f_sent()
    ss, pv = bv.at[:, 0], bv.at[:, 1]

    def s_copy(dx, dy):
        at = rel(dx, dy)
        return remote(ss.at[at], sr.at[at], g_send.at[at], g_recv.at[at], env.sibling)

    def grads(dx, dy):
        chip = env.chip(dx, dy)
        cx, cy = mod4(x, dx), mod4(y, dy)
        for cc in (0, 1):
            full = jnp.dot(
                gt[...],
                xv[:, pl.ds(pl.multiple_of(chip * 512 + cc * 256, 256), 256)],
                preferred_element_type=F32,
            ).astype(BF16)
            for q in range(16):
                dense[cc, q] = full[q % 8 * BLK:(q % 8 + 1) * BLK, q // 8 * BLK:(q // 8 + 1) * BLK]
        for out, cc in ((ss, 1 - core), (pv, core)):
            for s in range(CAP):
                out[rel(dx, dy), s * BLK:(s + 1) * BLK, :] = dense[cc, idxs[cc, cy, cx, z, 0, s]]
        go(s_copy(dx, dy))

    def merge(dx, dy):
        s_copy(dx, dy).wait_recv()
        at = rel(dx, dy)
        pv[at] = (pv[at].astype(F32) + sr[at].astype(F32)).astype(BF16)

    def lane_off(lane, du, dv_):
        return (du, dv_) if lane == 0 else (dv_, du)

    def rows_of(lane, q0, nq):
        return pl.ds((lane * 2 + q0) * 192, nq * 192)

    def hop(lane, axis, sign):
        return env.peer(*lane_off(lane, sign, 0)) if axis == 0 else env.peer(*lane_off(lane, 0, sign))

    def v1_copy(lane, k, side):
        at = rel(*lane_off(lane, U_OF_K[k], 2))
        n = lane * 16 + k * 4 + side
        return remote(
            pv.at[at, rows_of(lane, side, 1), :], rv1.at[lane, k, side], r_send.at[n], r_recv.at[n],
            hop(lane, 1, 1 - 2 * side),
        )

    def v2_copy(lane, k, side):
        at = rel(*lane_off(lane, U_OF_K[k], 1 - 2 * side))
        n = lane * 16 + k * 4 + 2 + side
        return remote(
            pv.at[at, rows_of(lane, 0, 2), :], rv2.at[lane, k, side], r_send.at[n], r_recv.at[n],
            hop(lane, 1, 1 - 2 * side),
        )

    def u1_copy(lane, side):
        at = rel(*lane_off(lane, 2, 0))
        n = 32 + lane * 4 + side
        return remote(
            pv.at[at, rows_of(lane, side, 1), :], ru1.at[lane, side], r_send.at[n], r_recv.at[n],
            hop(lane, 0, 1 - 2 * side),
        )

    def u2_copy(lane, side):
        at = rel(*lane_off(lane, 1 - 2 * side, 0))
        n = 32 + lane * 4 + 2 + side
        return remote(
            pv.at[at, rows_of(lane, 0, 2), :], ru2.at[lane, side], r_send.at[n], r_recv.at[n],
            hop(lane, 0, 1 - 2 * side),
        )

    def add(at, lane, q0, nq, got):
        rows = rows_of(lane, q0, nq)
        pv[at, rows, :] = (pv[at, rows, :].astype(F32) + got.astype(F32)).astype(BF16)

    def rv_first(lane, k):
        for side in (0, 1):
            go(v1_copy(lane, k, side))

    def rv_second(lane, k):
        for side in (0, 1):
            v1_copy(lane, k, side).wait_recv()
            add(rel(*lane_off(lane, U_OF_K[k], 1 - 2 * side)), lane, side, 1, rv1[lane, k, side])
            go(v2_copy(lane, k, side))

    def rv_third(lane, k):
        for side in (0, 1):
            v2_copy(lane, k, side).wait_recv()
        at = rel(*lane_off(lane, U_OF_K[k], 0))
        add(at, lane, 0, 2, rv2[lane, k, 0].astype(F32) + rv2[lane, k, 1].astype(F32))

    def ru_first(lane):
        for side in (0, 1):
            go(u1_copy(lane, side))

    def ru_second(lane):
        for side in (0, 1):
            u1_copy(lane, side).wait_recv()
            add(rel(*lane_off(lane, 1 - 2 * side, 0)), lane, side, 1, ru1[lane, side])
            go(u2_copy(lane, side))

    def ru_third(lane):
        for side in (0, 1):
            u2_copy(lane, side).wait_recv()
        total = pv[0, rows_of(lane, 0, 2), :].astype(F32) + ru2[lane, 0].astype(F32) + ru2[lane, 1].astype(F32)
        for s in range(3):
            gout[lane * 3 + s, 0] = jnp.transpose(total[s * BLK:(s + 1) * BLK])

    lanes = lambda f, *a: [functools.partial(f, 0, *a), functools.partial(f, 1, *a)]
    after = {
        0: lanes(rv_first, 3),
        4: lanes(rv_first, 2) + lanes(rv_first, 1),
        6: lanes(rv_second, 3) + lanes(rv_first, 0),
        8: [],
        10: lanes(rv_second, 2) + lanes(rv_second, 1) + lanes(rv_third, 3) + lanes(ru_first),
        12: [],
        14: lanes(rv_second, 0) + lanes(rv_third, 2) + lanes(rv_third, 1) + lanes(ru_second),
    }
    for n, c in enumerate(GRAD_ORDER):
        grads(*c)
        if n > 0:
            merge(*GRAD_ORDER[n - 1])
            for f in after.get(n - 1, ()):
                f()
        if n == 10:
            d_forward(1)
    merge(*GRAD_ORDER[15])

    for n in range(4):
        grad_second(n, 0)
    for f in lanes(rv_third, 0):
        f()
    for n in range(4):
        grad_second(n, 1)
        grad_second(n, 3)
    d_last(1)
    for n in range(4):
        grad_second(n, 2)
    for n in range(16):
        at = slice(n * 128, (n + 1) * 128)
        iout[:, at] = (iacc[:, at] * (wcol[...] * scale)).astype(BF16)
    for f in lanes(ru_third):
        f()
    for c in env.started:
        c.wait_send()
    teach1.sent()


def handed_on(g_in, i_in, g_out, i_out):
    g_out[...] = g_in[...]
    i_out[...] = i_in[...]


def body(hidden_states, teacher_weight, student_blocks, block_index):
    any_spec = pl.BlockSpec(memory_space=pl.ANY)
    vmem_spec = pl.BlockSpec(memory_space=pltpu.VMEM)
    dma = pltpu.SemaphoreType.DMA
    block_grads, input_grad = pl.pallas_call(
        kernel,
        out_shape=(
            jax.ShapeDtypeStruct((CAP, 1, BLK, BLK), F32),
            jax.ShapeDtypeStruct((TOK, OWN_COLS), BF16),
        ),
        in_specs=[any_spec] * 3 + [pl.BlockSpec(memory_space=pltpu.SMEM)],
        out_specs=(vmem_spec, vmem_spec),
        scratch_shapes=[
            pltpu.VMEM((TOK, D), BF16),
            pltpu.VMEM((2, 16, 2, 256, HALF), BF16),
            pltpu.VMEM((16, 2, BROWS, BLK), BF16),
            pltpu.VMEM((3, 4, 2, BROWS, BLK), BF16),
            pltpu.VMEM((2, 4, 4, 4, 1, 128), jnp.int32),
            pltpu.SMEM((2, 4, 4, 4, 1, 128), jnp.int32),
            pltpu.VMEM((2, TOK, HALF), F32),
            pltpu.VMEM((2, TOK, HALF), F32),
            pltpu.VMEM((2, CAP + 1, BLK, BLK), BF16),
            pltpu.VMEM((512, COLS), BF16),
            pltpu.VMEM((2, 4, TOK, HALF), BF16),
            pltpu.VMEM((COLS, TOK), BF16),
            pltpu.VMEM((2, 17, BLK, BLK), BF16),
            pltpu.VMEM((16, BROWS, BLK), BF16),
            pltpu.VMEM((2, 4, 2, 192, BLK), BF16),
            pltpu.VMEM((2, 4, 2, 384, BLK), BF16),
            pltpu.VMEM((2, 2, 192, BLK), BF16),
            pltpu.VMEM((2, 2, 384, BLK), BF16),
            pltpu.VMEM((4, 8, TOK), F32),
            pltpu.VMEM((TOK, 128), F32),
            pltpu.VMEM((TOK, OWN_COLS), F32),
            dma((6,)),
            dma((3, 2, 20)),
            dma((3, 2, 20)),
            dma((3, 32)),
            dma((3, 32)),
            dma((10,)),
            dma((10,)),
            dma((2, 16)),
            dma((2, 12)),
            dma((3,)),
            dma((3,)),
            dma((2, 4)),
            dma((2, 4)),
            dma((3,)),
            dma((3,)),
            dma((16,)),
            dma((16,)),
            dma((40,)),
            dma((40,)),
        ],
        compiler_params=pltpu.CompilerParams(
            collective_id=0, has_side_effects=True, vmem_limit_bytes=63 * 1024 * 1024
        ),
        cost_estimate=pl.CostEstimate(flops=26 * 10**9, bytes_accessed=10 * 10**6, transcendentals=0),
    )(hidden_states, teacher_weight, student_blocks.reshape(BROWS, BLK), block_index.T)
    g_spec = pl.BlockSpec((2, 1, BLK, BLK), lambda n: (n, 0, 0, 0))
    i_spec = pl.BlockSpec((128, OWN_COLS), lambda n: (n, 0))
    return pl.pallas_call(
        handed_on,
        grid=(3,),
        out_shape=(
            jax.ShapeDtypeStruct((CAP, 1, BLK, BLK), F32),
            jax.ShapeDtypeStruct((TOK, OWN_COLS), BF16),
        ),
        in_specs=[g_spec, i_spec],
        out_specs=(g_spec, i_spec),
    )(block_grads, input_grad)


def solution(mesh):
    in_specs = (P("dp", None), P("dp", "tensor"), P("dp", "tensor", None, None), P("dp", "tensor"))
    out_specs = (P("dp", "tensor", None, None), P("dp", "tensor"))
    return jax.shard_map(body, mesh=mesh, in_specs=in_specs, out_specs=out_specs, check_vma=False)
```
